32 devices in a mesh: seq: 8 (over z, x), chan: 4 (over y, core).
Axes of the slice: x: 2, y: 2, z: 4, core: 2. Of those that a mesh axis runs over, the one named last changes fastest.
Arguments:
- inner_gate: bfloat16 [4096, 2048], P('seq', 'chan'), may hold values from -6 to 6
- values: bfloat16 [4096, 2048], P('seq', 'chan'), may hold values from -6 to 6
- outer_gate: bfloat16 [4096, 2048], P('seq', 'chan'), may hold values from -6 to 6
- filter_taps: float32 [4096, 2048], P('seq', 'chan'), may hold values from -0.09375 to 0.09375
- skip_gain: float32 [2048], P('chan'), may hold values from -4 to 4
- out_proj: bfloat16 [2048, 2048], P('chan'), may hold values from -0.125 to 0.125
Outputs:
- mixer_out: bfloat16 [4096, 2048], P('seq', 'chan')
The draws below stay inside these ranges and needn't reach their ends.
All inputs are finite; a program needn't handle non-finite values.
Results may differ from the reference program's by a relative error of at most 0.013.
Values may be sent and summed in bfloat16 or wider, within the bound.
A program may use at most 128 MiB of HBM per device.

```python
import math
import jax
import jax.numpy as jnp
from jax import lax

D = 2048
BLK = 128
TOK_DEV = 512
SEQ_LEN = 4096
N_SEQ = 8


def block_levels(stream_key, extent, shards, least, largest):
    gain = 1.0
    for position, shards_of in shards:
        draws = jax.random.uniform(jax.random.fold_in(jax.random.fold_in(stream_key, 6), position), (shards_of,), jnp.float32, least / len(shards), largest / len(shards))
        gain = gain * jnp.repeat(jnp.exp(draws), extent[position] // shards_of).reshape((-1,) + (1,) * (len(extent) - 1 - position))
    return gain


def bell_draw(rng, dims, width, limit, split=(), kind=jnp.bfloat16):
    values = width * jax.random.normal(rng, dims, jnp.float32)
    if split:
        values = values * block_levels(rng, dims, split, -0.22, 0.18)
    return jnp.clip(values, -limit, limit).astype(kind)


def setup_inputs(seed: int = 0) -> dict:
    seeds = jax.random.split(jax.random.key(seed), 7)
    return {
        "inner_gate": bell_draw(seeds[0], (SEQ_LEN, D), 1.0, 6.0, ((0, 8), (1, 4))),
        "values": bell_draw(seeds[1], (SEQ_LEN, D), 1.0, 6.0, ((0, 8), (1, 4))),
        "outer_gate": bell_draw(seeds[2], (SEQ_LEN, D), 1.0, 6.0, ((0, 8), (1, 4))),
        "filter_taps": bell_draw(seeds[3], (SEQ_LEN, D), SEQ_LEN ** -0.5, 0.09375, ((0, 8), (1, 4)), jnp.float32),
        "skip_gain": bell_draw(seeds[4], (D,), 1.0, 4.0, ((0, 4),), jnp.float32),
        "out_proj": bell_draw(seeds[5], (D, D), D ** -0.5, 0.125, ((0, 4),)),
    }


def wave_table(length, direction):
    positions = jnp.arange(length, dtype=jnp.int32)
    phases = (positions[:, None] * positions[None, :]) % length
    angles = phases.astype(jnp.float32) * (2.0 * math.pi / length)
    return jnp.cos(angles).astype(jnp.bfloat16), (direction * jnp.sin(angles)).astype(jnp.bfloat16)


def twiddle(row_ids, col_ids, length, direction):
    phases = (row_ids * col_ids) % length
    angles = phases.astype(jnp.float32) * (2.0 * math.pi / length)
    return jnp.cos(angles), direction * jnp.sin(angles)


def wide_einsum(pattern, left, right):
    return jnp.einsum(pattern, left.astype(jnp.float32), right.astype(jnp.float32), precision=lax.Precision.HIGHEST)


def apply_table(pattern, table, signal):
    table_real, table_imag = table
    signal_real, signal_imag = signal
    out_real = wide_einsum(pattern, table_real, signal_real)
    out_imag = wide_einsum(pattern, table_imag, signal_real)
    if signal_imag is not None:
        out_real = out_real - wide_einsum(pattern, table_imag, signal_imag)
        out_imag = out_imag + wide_einsum(pattern, table_real, signal_imag)
    return out_real, out_imag


def twist_round(signal, factor):
    signal_real, signal_imag = signal
    factor_real, factor_imag = factor
    return ((signal_real * factor_real - signal_imag * factor_imag).astype(jnp.bfloat16),
            (signal_real * factor_imag + signal_imag * factor_real).astype(jnp.bfloat16))


def finish_forward(signal, tables, second):
    table_q, table_m = tables
    shaped = twist_round(apply_table("qj,...qmc->...jmc", table_q, signal), second)
    return apply_table("mn,...jmc->...jnc", table_m, shaped)


def start_inverse(spectrum, tables, second, first):
    table_q, table_m = tables
    shaped = twist_round(apply_table("mn,...jnc->...jmc", table_m, spectrum), second)
    return twist_round(apply_table("qj,...jmc->...qmc", table_q, shaped), first)


def combine(even_part, odd_part, half_cos, half_sin, seq_length):
    return (even_part[0] + (half_cos * odd_part[0] - half_sin * odd_part[1])) / (2.0 * seq_length)


def reference(inner_gate, values, outer_gate, filter_taps, skip_gain, out_proj):
    seq_length = SEQ_LEN
    lane_count = N_SEQ
    outer_count = TOK_DEV // BLK
    channels = inner_gate.shape[1]
    chan_block = min(channels, 128)
    slab_count = channels // chan_block
    forward_lane = wave_table(lane_count, -1.0)
    inverse_lane = wave_table(lane_count, 1.0)
    forward_local = (wave_table(outer_count, -1.0), wave_table(BLK, -1.0))
    inverse_local = (wave_table(outer_count, 1.0), wave_table(BLK, 1.0))
    outer_index = jnp.arange(outer_count, dtype=jnp.int32).reshape(outer_count, 1, 1)
    inner_index = jnp.arange(BLK, dtype=jnp.int32).reshape(1, BLK, 1)
    second_forward = twiddle(outer_index, inner_index, TOK_DEV, -1.0)
    second_inverse = twiddle(outer_index, inner_index, TOK_DEV, 1.0)
    lane_index = jnp.arange(lane_count, dtype=jnp.int32).reshape(lane_count, 1, 1, 1)
    row_index = jnp.arange(TOK_DEV, dtype=jnp.int32).reshape(1, outer_count, BLK, 1)
    first_forward = twiddle(lane_index, row_index, seq_length, -1.0)
    first_inverse = twiddle(lane_index, row_index, seq_length, 1.0)
    time_angle = jnp.arange(seq_length, dtype=jnp.int32).astype(jnp.float32).reshape(seq_length, 1) * (math.pi / seq_length)
    own_cos = jnp.cos(time_angle)
    own_sin = jnp.sin(time_angle)
    lane_cos = own_cos.reshape(lane_count, outer_count, BLK, 1)
    lane_sin = own_sin.reshape(lane_count, outer_count, BLK, 1)

    def split_slabs(array):
        return array.reshape(seq_length, slab_count, chan_block).transpose(1, 0, 2)

    def one_block(pieces):
        inner_part, value_part, outer_part, taps_part, skip_part = pieces
        mixed = (inner_part.astype(jnp.float32) * value_part.astype(jnp.float32)).astype(jnp.bfloat16)
        mixed = lax.optimization_barrier(mixed)
        mixed_wide = mixed.astype(jnp.float32)
        odd_real = (mixed_wide * own_cos).astype(jnp.bfloat16)
        odd_imag = (-(mixed_wide * own_sin)).astype(jnp.bfloat16)
        taps_even = taps_part.astype(jnp.bfloat16)
        taps_real = (taps_part * own_cos).astype(jnp.bfloat16)
        taps_imag = (-(taps_part * own_sin)).astype(jnp.bfloat16)
        shape_four = (lane_count, outer_count, BLK, chan_block)
        signals = ((mixed.reshape(shape_four), None),
                   (odd_real.reshape(shape_four), odd_imag.reshape(shape_four)),
                   (taps_even.reshape(shape_four), None),
                   (taps_real.reshape(shape_four), taps_imag.reshape(shape_four)))
        spectra = [finish_forward(twist_round(apply_table("pk,p...->k...", forward_lane, signal), first_forward),
                                  forward_local, second_forward) for signal in signals]
        product_even = twist_round(spectra[0], spectra[2])
        product_odd = twist_round(spectra[1], spectra[3])
        back_even = start_inverse(product_even, inverse_local, second_inverse, first_inverse)
        back_odd = start_inverse(product_odd, inverse_local, second_inverse, first_inverse)
        even_part = apply_table("pk,k...->p...", inverse_lane, back_even)
        odd_part = apply_table("pk,k...->p...", inverse_lane, back_odd)
        convolved = combine(even_part, odd_part, lane_cos, lane_sin, seq_length).reshape(seq_length, chan_block)
        return (outer_part.astype(jnp.float32) * (convolved + skip_part[None, :] * value_part.astype(jnp.float32))).astype(jnp.bfloat16)

    gated = lax.map(one_block, (split_slabs(inner_gate), split_slabs(values), split_slabs(outer_gate),
                                split_slabs(filter_taps), skip_gain.reshape(slab_count, chan_block)))
    gated = gated.transpose(1, 0, 2).reshape(seq_length, channels)
    return jnp.dot(gated, out_proj, preferred_element_type=jnp.float32).astype(jnp.bfloat16)
```

```python
import functools
import math

import jax
import jax.numpy as jnp
import numpy as np
from jax import lax
from jax.experimental import pallas as pl
from jax.experimental.pallas import tpu as pltpu
from jax.sharding import PartitionSpec as P

BLK = 128


def wave_table(length, direction):
    positions = jnp.arange(length, dtype=jnp.int32)
    phases = positions[:, None] * positions[None, :] % length
    angles = phases.astype(jnp.float32) * (2.0 * math.pi / length)
    return (
        jnp.cos(angles).astype(jnp.bfloat16),
        (direction * jnp.sin(angles)).astype(jnp.bfloat16),
    )


def twiddle(row_ids, col_ids, length, direction):
    phases = row_ids * col_ids % length
    angles = phases.astype(jnp.float32) * (2.0 * math.pi / length)
    return (jnp.cos(angles), direction * jnp.sin(angles))


def apply_table(pattern, table, signal):
    table_real, table_imag = table
    signal_real, signal_imag = signal
    out_real = jnp.einsum(pattern, table_real, signal_real, preferred_element_type=jnp.float32)
    out_imag = jnp.einsum(pattern, table_imag, signal_real, preferred_element_type=jnp.float32)
    if signal_imag is not None:
        out_real = out_real - jnp.einsum(
            pattern, table_imag, signal_imag, preferred_element_type=jnp.float32
        )
        out_imag = out_imag + jnp.einsum(
            pattern, table_real, signal_imag, preferred_element_type=jnp.float32
        )
    return (out_real, out_imag)


def twist_round(signal, factor):
    signal_real, signal_imag = signal
    factor_real, factor_imag = factor
    return (
        (signal_real * factor_real - signal_imag * factor_imag).astype(jnp.bfloat16),
        (signal_real * factor_imag + signal_imag * factor_real).astype(jnp.bfloat16),
    )


def lead_forward(signal, lane_table, first, tables, second):
    table_q, table_m = tables
    section = twist_round(apply_table("pk,cpqm->ckqm", lane_table, signal), first)
    shaped = twist_round(apply_table("qj,ckqm->ckjm", table_q, section), second)
    return apply_table("mn,ckjm->ckjn", table_m, shaped)


def lead_inverse(spectrum, tables, second, first):
    table_q, table_m = tables
    shaped = twist_round(apply_table("mn,ckjn->ckjm", table_m, spectrum), second)
    return twist_round(apply_table("qj,ckjm->ckqm", table_q, shaped), first)


def combine(even_part, odd_part, half_cos, half_sin, seq_length):
    return (even_part[0] + (half_cos * odd_part[0] - half_sin * odd_part[1])) / (2.0 * seq_length)


def plain_on_device(inner_gate, values, outer_gate, filter_taps, skip_gain, out_proj):
    seq_count = lax.axis_size("seq")
    my_index = lax.axis_index("seq")
    tokens = inner_gate.shape[0]
    seq_length = tokens * seq_count
    block_count = tokens // BLK
    forward_lane = wave_table(seq_count, -1.0)
    inverse_lane = wave_table(seq_count, 1.0)
    forward_local = (wave_table(block_count, -1.0), wave_table(BLK, -1.0))
    inverse_local = (wave_table(block_count, 1.0), wave_table(BLK, 1.0))
    own_angle = (my_index * tokens + jnp.arange(tokens, dtype=jnp.int32)).astype(
        jnp.float32
    ).reshape(tokens, 1) * (math.pi / seq_length)
    own_cos = jnp.cos(own_angle)
    own_sin = jnp.sin(own_angle)
    mixed = (inner_gate.astype(jnp.float32) * values.astype(jnp.float32)).astype(jnp.bfloat16)
    mixed = lax.optimization_barrier(mixed)
    mixed_wide = mixed.astype(jnp.float32)
    odd_real = (mixed_wide * own_cos).astype(jnp.bfloat16)
    odd_imag = (-(mixed_wide * own_sin)).astype(jnp.bfloat16)
    taps_even = filter_taps.astype(jnp.bfloat16)
    taps_real = (filter_taps * own_cos).astype(jnp.bfloat16)
    taps_imag = (-(filter_taps * own_sin)).astype(jnp.bfloat16)
    spread = (
        lax.all_to_all(mixed, "seq", split_axis=1, concat_axis=0, tiled=True),
        lax.all_to_all(odd_real, "seq", split_axis=1, concat_axis=0, tiled=True),
        lax.all_to_all(odd_imag, "seq", split_axis=1, concat_axis=0, tiled=True),
        lax.all_to_all(taps_even, "seq", split_axis=1, concat_axis=0, tiled=True),
        lax.all_to_all(taps_real, "seq", split_axis=1, concat_axis=0, tiled=True),
        lax.all_to_all(taps_imag, "seq", split_axis=1, concat_axis=0, tiled=True),
    )
    slab_width = spread[0].shape[1]
    slabs = [piece.T.reshape(slab_width, seq_count, block_count, BLK) for piece in spread]
    outer_flat = jnp.arange(block_count, dtype=jnp.int32).reshape(block_count, 1)
    inner_flat = jnp.arange(BLK, dtype=jnp.int32).reshape(1, BLK)
    second_forward = twiddle(outer_flat, inner_flat, tokens, -1.0)
    second_inverse = twiddle(outer_flat, inner_flat, tokens, 1.0)
    lane_index = jnp.arange(seq_count, dtype=jnp.int32).reshape(seq_count, 1, 1)
    row_index = jnp.arange(tokens, dtype=jnp.int32).reshape(1, block_count, BLK)
    first_forward = twiddle(lane_index, row_index, seq_length, -1.0)
    first_inverse = twiddle(lane_index, row_index, seq_length, 1.0)
    signals = ((slabs[0], None), (slabs[1], slabs[2]), (slabs[3], None), (slabs[4], slabs[5]))
    spectra = [
        lead_forward(signal, forward_lane, first_forward, forward_local, second_forward)
        for signal in signals
    ]
    product_even = twist_round(spectra[0], spectra[2])
    product_odd = twist_round(spectra[1], spectra[3])
    back_even = lead_inverse(product_even, inverse_local, second_inverse, first_inverse)
    back_odd = lead_inverse(product_odd, inverse_local, second_inverse, first_inverse)
    even_part = apply_table("pk,ckqm->cpqm", inverse_lane, back_even)
    odd_part = apply_table("pk,ckqm->cpqm", inverse_lane, back_odd)
    lane_angle = (lane_index * tokens + row_index).astype(jnp.float32) * (math.pi / seq_length)
    slab_conv = combine(even_part, odd_part, jnp.cos(lane_angle), jnp.sin(lane_angle), seq_length)
    slab_conv = slab_conv.reshape(slab_width, seq_length).T
    convolved = lax.all_to_all(
        slab_conv.astype(jnp.bfloat16), "seq", split_axis=0, concat_axis=1, tiled=True
    ).astype(slab_conv.dtype)
    gated = (
        outer_gate.astype(jnp.float32)
        * (convolved + skip_gain[None, :] * values.astype(jnp.float32))
    ).astype(jnp.bfloat16)
    partial_value = jnp.dot(gated, out_proj, preferred_element_type=jnp.float32)
    return lax.psum_scatter(
        partial_value.astype(jnp.bfloat16), "chan", scatter_dimension=1, tiled=True
    )


SHIFT = 0.25
MESH = pl.DeviceIdType.MESH


def split_forward(pieces):
    count = len(pieces)
    if count == 1:
        return [(pieces[0], None)]
    even, odd = split_forward(pieces[0::2]), split_forward(pieces[1::2])
    low, high = [], []
    for k in range(count // 2):
        angle = 2.0 * math.pi * (k + SHIFT) / count
        cos, sin = math.cos(angle), math.sin(angle)
        odd_re, odd_im = odd[k]
        even_re, even_im = even[k]
        if odd_im is None:
            turn_re, turn_im = cos * odd_re, -sin * odd_re
            low.append((even_re + turn_re, turn_im))
            high.append((even_re - turn_re, -turn_im))
        else:
            turn_re = cos * odd_re + sin * odd_im
            turn_im = cos * odd_im - sin * odd_re
            low.append((even_re + turn_re, even_im + turn_im))
            high.append((even_re - turn_re, even_im - turn_im))
    return low + high


def split_inverse(bins):
    count = len(bins)
    if count == 1:
        return [bins[0][0]]
    half = count // 2
    even, odd = [], []
    for k in range(half):
        angle = 2.0 * math.pi * (k + SHIFT) / count
        cos, sin = math.cos(angle), math.sin(angle)
        (low_re, low_im), (high_re, high_im) = bins[k], bins[k + half]
        gap_re, gap_im = low_re - high_re, low_im - high_im
        if half == 1:
            even.append((low_re + high_re, None))
            odd.append((cos * gap_re - sin * gap_im, None))
        else:
            even.append((low_re + high_re, low_im + high_im))
            odd.append((cos * gap_re - sin * gap_im, sin * gap_re + cos * gap_im))
    even, odd = split_inverse(even), split_inverse(odd)
    return [piece for pair in zip(even, odd) for piece in pair]


def mixer_kernel(
    lanes,
    groups,
    inner_ref,
    values_ref,
    outer_ref,
    taps_ref,
    skip_ref,
    proj_ref,
    cos_ref,
    sin_ref,
    turn_cos_ref,
    turn_sin_ref,
    out_ref,
    leave,
    arrive,
    sec_re,
    sec_im,
    back_re,
    back_im,
    conv_leave,
    conv_arrive,
    gathered,
    weights,
    total,
    in_send,
    in_recv,
    conv_send,
    conv_recv,
    side_send,
    side_recv,
    proj_send,
    proj_recv,
    proj_own,
):
    me = lax.axis_index("seq")
    slab = lax.axis_index("chan")
    slabs = 4
    tokens = inner_ref.shape[0]
    wide = inner_ref.shape[1] // groups
    each = wide // lanes
    columns = out_ref.shape[1]
    sibling = slab + 1 - 2 * (slab % 2)
    across = (slab + 2) % 4
    corner = (sibling + 2) % 4

    barrier = pltpu.get_barrier_semaphore()

    @pl.loop(1, lanes)
    def _(step):
        pl.semaphore_signal(
            barrier, inc=1, device_id={"seq": (me + step) % lanes}, device_id_type=MESH
        )

    for step in range(1, slabs):
        pl.semaphore_signal(
            barrier, inc=1, device_id={"chan": (slab + step) % slabs}, device_id_type=MESH
        )

    def prepare(g):
        cols = pl.ds(pl.multiple_of(g * wide, wide), wide)
        mixed = inner_ref[:, cols].astype(jnp.float32) * values_ref[:, cols].astype(jnp.float32)
        mixed = mixed.T.astype(jnp.bfloat16)
        taps = taps_ref[:, cols].T.astype(jnp.bfloat16)
        for p in range(lanes):
            leave[g, p, 0] = mixed[p * each : (p + 1) * each, :]
            leave[g, p, 1] = taps[p * each : (p + 1) * each, :]
        arrive[g, me] = leave[g, me]

    def in_copy(g, step, source):
        target = (me + step) % lanes
        return pltpu.make_async_remote_copy(
            src_ref=leave.at[g, target],
            dst_ref=arrive.at[g, source],
            send_sem=in_send.at[g, step],
            recv_sem=in_recv.at[g, step],
            device_id={"seq": target},
            device_id_type=MESH,
        )

    def conv_copy(g, step, source):
        target = (me + step) % lanes
        return pltpu.make_async_remote_copy(
            src_ref=conv_leave.at[g, target],
            dst_ref=conv_arrive.at[g, source],
            send_sem=conv_send.at[g, step],
            recv_sem=conv_recv.at[g, step],
            device_id={"seq": target},
            device_id_type=MESH,
        )

    def proj_copy(step, source):
        target = (slab + step) % slabs
        return pltpu.make_async_remote_copy(
            src_ref=proj_ref.at[:, :, pl.ds(pl.multiple_of(target * columns, columns), columns)],
            dst_ref=weights.at[:, source],
            send_sem=proj_send.at[step],
            recv_sem=proj_recv.at[step],
            device_id={"chan": target},
            device_id_type=MESH,
        )

    def side_copy(g, kind, block, target):
        return pltpu.make_async_remote_copy(
            src_ref=gathered.at[g, block],
            dst_ref=gathered.at[g, block],
            send_sem=side_send.at[g, kind],
            recv_sem=side_recv.at[g, kind],
            device_id={"chan": target},
            device_id_type=MESH,
        )

    prepare(0)
    pl.semaphore_wait(barrier, lanes - 1 + slabs - 1)

    own_proj = pltpu.make_async_copy(
        proj_ref.at[:, :, pl.ds(pl.multiple_of(slab * columns, columns), columns)],
        weights.at[:, slab],
        proj_own,
    )

    @pl.loop(1, lanes)
    def _(step):
        in_copy(0, step, me).start()

    own_proj.start()
    for step in range(1, slabs):
        proj_copy(step, slab).start()

    @pl.loop(1, groups)
    def _(g):
        prepare(g)

        @pl.loop(1, lanes)
        def _(step):
            in_copy(g, step, me).start()

    def dot(left, right):
        return jnp.dot(left, right, preferred_element_type=jnp.float32)

    @pl.loop(0, groups)
    def _(g):
        @pl.loop(1, lanes)
        def _(step):
            in_copy(g, step, (me + lanes - step) % lanes).wait_recv()

        @pl.loop(0, tokens // BLK)
        def _(j):
            span = pl.ds(pl.multiple_of(j * BLK, BLK), BLK)
            for sig in range(2):
                bins = split_forward(
                    [arrive[g, p, sig, :, span].astype(jnp.float32) for p in range(lanes)]
                )
                for k in range(lanes):
                    re, im = bins[k]
                    cos, sin = turn_cos_ref[k : k + 1, span], turn_sin_ref[k : k + 1, span]
                    sec_re[sig, k, :, span] = (re * cos + im * sin).astype(jnp.bfloat16)
                    sec_im[sig, k, :, span] = (im * cos - re * sin).astype(jnp.bfloat16)

        rows = lanes * each
        re = sec_re[...].reshape(2 * rows, tokens)
        im = sec_im[...].reshape(2 * rows, tokens)
        cos, sin = cos_ref[...], sin_ref[...]
        spec_re = dot(re, cos) + dot(im, sin)
        spec_im = dot(im, cos) - dot(re, sin)
        x_re, h_re = spec_re[:rows], spec_re[rows:]
        x_im, h_im = spec_im[:rows], spec_im[rows:]
        prod_re = (x_re * h_re - x_im * h_im).astype(jnp.bfloat16)
        prod_im = (x_re * h_im + x_im * h_re).astype(jnp.bfloat16)
        back_re[...] = (dot(prod_re, cos) - dot(prod_im, sin)).reshape(lanes, each, tokens)
        back_im[...] = (dot(prod_im, cos) + dot(prod_re, sin)).reshape(lanes, each, tokens)

        @pl.loop(0, tokens // BLK)
        def _(j):
            span = pl.ds(pl.multiple_of(j * BLK, BLK), BLK)
            bins = []
            for k in range(lanes):
                re, im = back_re[k, :, span], back_im[k, :, span]
                cos, sin = turn_cos_ref[k : k + 1, span], turn_sin_ref[k : k + 1, span]
                bins.append((re * cos - im * sin, re * sin + im * cos))
            pieces = split_inverse(bins)
            for p in range(lanes):
                conv_leave[g, p, :, span] = (pieces[p] * (1.0 / (lanes * tokens))).astype(
                    jnp.bfloat16
                )

        @pl.loop(1, lanes)
        def _(step):
            conv_copy(g, step, me).start()

        conv_arrive[g, me] = conv_leave[g, me]

    def forward(g):
        side_copy(g, 1, across, across).wait_recv()
        side_copy(g, 2, across, sibling).start()

    for g in range(groups):

        @pl.loop(1, lanes)
        def _(step):
            conv_copy(g, step, (me + lanes - step) % lanes).wait_recv()

        cols = slice(g * wide, (g + 1) * wide)
        conv = conv_arrive[g].astype(jnp.float32).reshape(wide, tokens).T
        gated = outer_ref[:, cols].astype(jnp.float32) * (
            conv + skip_ref[:, cols] * values_ref[:, cols].astype(jnp.float32)
        )
        gathered[g, slab] = gated.astype(jnp.bfloat16)
        side_copy(g, 1, slab, across).start()
        side_copy(g, 0, slab, sibling).start()
        if g > 0:
            forward(g - 1)
    forward(groups - 1)

    own_proj.wait()
    for step in range(1, slabs):
        proj_copy(step, (slab + slabs - step) % slabs).wait_recv()

    for g in range(groups):
        side_copy(g, 0, sibling, sibling).wait_recv()
        side_copy(g, 2, corner, sibling).wait_recv()
        left = jnp.concatenate([gathered[g, j] for j in range(slabs)], axis=1)
        part = dot(left, weights[g].reshape(slabs * wide, columns))
        if g == 0:
            total[...] = part
        elif g < groups - 1:
            total[...] += part
        else:
            out_ref[...] = (total[...] + part).astype(out_ref.dtype)

    @pl.loop(0, groups)
    def _(g):
        @pl.loop(1, lanes)
        def _(step):
            in_copy(g, step, me).wait_send()
            conv_copy(g, step, me).wait_send()

        side_copy(g, 0, slab, sibling).wait_send()
        side_copy(g, 1, slab, across).wait_send()
        side_copy(g, 2, across, sibling).wait_send()

    for step in range(1, slabs):
        proj_copy(step, slab).wait_send()


def kernel_on_device(lanes, groups, inner_gate, values, outer_gate, filter_taps, skip_gain, out_proj):
    slabs = 4
    tokens, channels = inner_gate.shape
    wide = channels // groups
    each = wide // lanes
    columns = out_proj.shape[1] // slabs
    index = np.arange(tokens)
    angles = 2.0 * np.pi * ((index[:, None] * index[None, :]) % tokens) / tokens
    turns = 2.0 * np.pi * (np.arange(lanes)[:, None] + SHIFT) * index[None, :] / (lanes * tokens)
    tables = (
        jnp.asarray(np.cos(angles), jnp.bfloat16),
        jnp.asarray(np.sin(angles), jnp.bfloat16),
        jnp.asarray(np.cos(turns), jnp.float32),
        jnp.asarray(np.sin(turns), jnp.float32),
    )
    here = pl.BlockSpec(memory_space=pltpu.VMEM)
    dma = pltpu.SemaphoreType.DMA
    return pl.pallas_call(
        functools.partial(mixer_kernel, lanes, groups),
        out_shape=jax.ShapeDtypeStruct((tokens, columns), jnp.bfloat16),
        in_specs=[here] * 5 + [pl.BlockSpec(memory_space=pl.ANY)] + [here] * 4,
        out_specs=here,
        scratch_shapes=[
            pltpu.VMEM((groups, lanes, 2, each, tokens), jnp.bfloat16),
            pltpu.VMEM((groups, lanes, 2, each, tokens), jnp.bfloat16),
            pltpu.VMEM((2, lanes, each, tokens), jnp.bfloat16),
            pltpu.VMEM((2, lanes, each, tokens), jnp.bfloat16),
            pltpu.VMEM((lanes, each, tokens), jnp.float32),
            pltpu.VMEM((lanes, each, tokens), jnp.float32),
            pltpu.VMEM((groups, lanes, each, tokens), jnp.bfloat16),
            pltpu.VMEM((groups, lanes, each, tokens), jnp.bfloat16),
            pltpu.VMEM((groups, slabs, tokens, wide), jnp.bfloat16),
            pltpu.VMEM((groups, slabs, wide, columns), jnp.bfloat16),
            pltpu.VMEM((tokens, columns), jnp.float32),
            dma((groups, lanes)),
            dma((groups, lanes)),
            dma((groups, lanes)),
            dma((groups, lanes)),
            dma((groups, 3)),
            dma((groups, 3)),
            dma((slabs,)),
            dma((slabs,)),
            dma,
        ],
        compiler_params=pltpu.CompilerParams(
            collective_id=0, has_side_effects=True, vmem_limit_bytes=48 * 1024 * 1024
        ),
    )(
        inner_gate,
        values,
        outer_gate,
        filter_taps,
        skip_gain.reshape(1, channels),
        out_proj.reshape(groups, wide, out_proj.shape[1]),
        *tables,
    )


def on_device(inner_gate, *others):
    lanes = lax.axis_size("seq")
    tokens, channels = inner_gate.shape
    groups = channels // (16 * lanes)
    fits = (
        lax.axis_size("chan") == 4
        and groups >= 2
        and channels == groups * 16 * lanes
        and lanes % 8 == 0
        and tokens % BLK == 0
        and lanes & (lanes - 1) == 0
    )
    if fits:
        return kernel_on_device(lanes, groups, inner_gate, *others)
    return plain_on_device(inner_gate, *others)


def solution(mesh):
    return jax.shard_map(
        on_device,
        mesh=mesh,
        in_specs=(
            P("seq", "chan"),
            P("seq", "chan"),
            P("seq", "chan"),
            P("seq", "chan"),
            P("chan"),
            P("chan", None),
        ),
        out_specs=P("seq", "chan"),
        check_vma=False,
    )
```

```python
import functools
import math

import jax
import jax.numpy as jnp
import numpy as np
from jax import lax
from jax.experimental import pallas as pl
from jax.experimental.pallas import tpu as pltpu
from jax.sharding import PartitionSpec as P

BLK = 128


def wave_table(length, direction):
    positions = jnp.arange(length, dtype=jnp.int32)
    phases = positions[:, None] * positions[None, :] % length
    angles = phases.astype(jnp.float32) * (2.0 * math.pi / length)
    return (
        jnp.cos(angles).astype(jnp.bfloat16),
        (direction * jnp.sin(angles)).astype(jnp.bfloat16),
    )


def twiddle(row_ids, col_ids, length, direction):
    phases = row_ids * col_ids % length
    angles = phases.astype(jnp.float32) * (2.0 * math.pi / length)
    return (jnp.cos(angles), direction * jnp.sin(angles))


def apply_table(pattern, table, signal):
    table_real, table_imag = table
    signal_real, signal_imag = signal
    out_real = jnp.einsum(pattern, table_real, signal_real, preferred_element_type=jnp.float32)
    out_imag = jnp.einsum(pattern, table_imag, signal_real, preferred_element_type=jnp.float32)
    if signal_imag is not None:
        out_real = out_real - jnp.einsum(
            pattern, table_imag, signal_imag, preferred_element_type=jnp.float32
        )
        out_imag = out_imag + jnp.einsum(
            pattern, table_real, signal_imag, preferred_element_type=jnp.float32
        )
    return (out_real, out_imag)


def twist_round(signal, factor):
    signal_real, signal_imag = signal
    factor_real, factor_imag = factor
    return (
        (signal_real * factor_real - signal_imag * factor_imag).astype(jnp.bfloat16),
        (signal_real * factor_imag + signal_imag * factor_real).astype(jnp.bfloat16),
    )


def lead_forward(signal, lane_table, first, tables, second):
    table_q, table_m = tables
    section = twist_round(apply_table("pk,cpqm->ckqm", lane_table, signal), first)
    shaped = twist_round(apply_table("qj,ckqm->ckjm", table_q, section), second)
    return apply_table("mn,ckjm->ckjn", table_m, shaped)


def lead_inverse(spectrum, tables, second, first):
    table_q, table_m = tables
    shaped = twist_round(apply_table("mn,ckjn->ckjm", table_m, spectrum), second)
    return twist_round(apply_table("qj,ckjm->ckqm", table_q, shaped), first)


def combine(even_part, odd_part, half_cos, half_sin, seq_length):
    return (even_part[0] + (half_cos * odd_part[0] - half_sin * odd_part[1])) / (2.0 * seq_length)


def plain_on_device(inner_gate, values, outer_gate, filter_taps, skip_gain, out_proj):
    seq_count = lax.axis_size("seq")
    my_index = lax.axis_index("seq")
    tokens = inner_gate.shape[0]
    seq_length = tokens * seq_count
    block_count = tokens // BLK
    forward_lane = wave_table(seq_count, -1.0)
    inverse_lane = wave_table(seq_count, 1.0)
    forward_local = (wave_table(block_count, -1.0), wave_table(BLK, -1.0))
    inverse_local = (wave_table(block_count, 1.0), wave_table(BLK, 1.0))
    own_angle = (my_index * tokens + jnp.arange(tokens, dtype=jnp.int32)).astype(
        jnp.float32
    ).reshape(tokens, 1) * (math.pi / seq_length)
    own_cos = jnp.cos(own_angle)
    own_sin = jnp.sin(own_angle)
    mixed = (inner_gate.astype(jnp.float32) * values.astype(jnp.float32)).astype(jnp.bfloat16)
    mixed = lax.optimization_barrier(mixed)
    mixed_wide = mixed.astype(jnp.float32)
    odd_real = (mixed_wide * own_cos).astype(jnp.bfloat16)
    odd_imag = (-(mixed_wide * own_sin)).astype(jnp.bfloat16)
    taps_even = filter_taps.astype(jnp.bfloat16)
    taps_real = (filter_taps * own_cos).astype(jnp.bfloat16)
    taps_imag = (-(filter_taps * own_sin)).astype(jnp.bfloat16)
    spread = (
        lax.all_to_all(mixed, "seq", split_axis=1, concat_axis=0, tiled=True),
        lax.all_to_all(odd_real, "seq", split_axis=1, concat_axis=0, tiled=True),
        lax.all_to_all(odd_imag, "seq", split_axis=1, concat_axis=0, tiled=True),
        lax.all_to_all(taps_even, "seq", split_axis=1, concat_axis=0, tiled=True),
        lax.all_to_all(taps_real, "seq", split_axis=1, concat_axis=0, tiled=True),
        lax.all_to_all(taps_imag, "seq", split_axis=1, concat_axis=0, tiled=True),
    )
    slab_width = spread[0].shape[1]
    slabs = [piece.T.reshape(slab_width, seq_count, block_count, BLK) for piece in spread]
    outer_flat = jnp.arange(block_count, dtype=jnp.int32).reshape(block_count, 1)
    inner_flat = jnp.arange(BLK, dtype=jnp.int32).reshape(1, BLK)
    second_forward = twiddle(outer_flat, inner_flat, tokens, -1.0)
    second_inverse = twiddle(outer_flat, inner_flat, tokens, 1.0)
    lane_index = jnp.arange(seq_count, dtype=jnp.int32).reshape(seq_count, 1, 1)
    row_index = jnp.arange(tokens, dtype=jnp.int32).reshape(1, block_count, BLK)
    first_forward = twiddle(lane_index, row_index, seq_length, -1.0)
    first_inverse = twiddle(lane_index, row_index, seq_length, 1.0)
    signals = ((slabs[0], None), (slabs[1], slabs[2]), (slabs[3], None), (slabs[4], slabs[5]))
    spectra = [
        lead_forward(signal, forward_lane, first_forward, forward_local, second_forward)
        for signal in signals
    ]
    product_even = twist_round(spectra[0], spectra[2])
    product_odd = twist_round(spectra[1], spectra[3])
    back_even = lead_inverse(product_even, inverse_local, second_inverse, first_inverse)
    back_odd = lead_inverse(product_odd, inverse_local, second_inverse, first_inverse)
    even_part = apply_table("pk,ckqm->cpqm", inverse_lane, back_even)
    odd_part = apply_table("pk,ckqm->cpqm", inverse_lane, back_odd)
    lane_angle = (lane_index * tokens + row_index).astype(jnp.float32) * (math.pi / seq_length)
    slab_conv = combine(even_part, odd_part, jnp.cos(lane_angle), jnp.sin(lane_angle), seq_length)
    slab_conv = slab_conv.reshape(slab_width, seq_length).T
    convolved = lax.all_to_all(
        slab_conv.astype(jnp.bfloat16), "seq", split_axis=0, concat_axis=1, tiled=True
    ).astype(slab_conv.dtype)
    gated = (
        outer_gate.astype(jnp.float32)
        * (convolved + skip_gain[None, :] * values.astype(jnp.float32))
    ).astype(jnp.bfloat16)
    partial_value = jnp.dot(gated, out_proj, preferred_element_type=jnp.float32)
    return lax.psum_scatter(
        partial_value.astype(jnp.bfloat16), "chan", scatter_dimension=1, tiled=True
    )


SHIFT = 0.25
MESH = pl.DeviceIdType.MESH


def split_forward(pieces):
    count = len(pieces)
    if count == 1:
        return [(pieces[0], None)]
    even, odd = split_forward(pieces[0::2]), split_forward(pieces[1::2])
    low, high = [], []
    for k in range(count // 2):
        angle = 2.0 * math.pi * (k + SHIFT) / count
        cos, sin = math.cos(angle), math.sin(angle)
        odd_re, odd_im = odd[k]
        even_re, even_im = even[k]
        if odd_im is None:
            turn_re, turn_im = cos * odd_re, -sin * odd_re
            low.append((even_re + turn_re, turn_im))
            high.append((even_re - turn_re, -turn_im))
        else:
            turn_re = cos * odd_re + sin * odd_im
            turn_im = cos * odd_im - sin * odd_re
            low.append((even_re + turn_re, even_im + turn_im))
            high.append((even_re - turn_re, even_im - turn_im))
    return low + high


def split_inverse(bins):
    count = len(bins)
    if count == 1:
        return [bins[0][0]]
    half = count // 2
    even, odd = [], []
    for k in range(half):
        angle = 2.0 * math.pi * (k + SHIFT) / count
        cos, sin = math.cos(angle), math.sin(angle)
        (low_re, low_im), (high_re, high_im) = bins[k], bins[k + half]
        gap_re, gap_im = low_re - high_re, low_im - high_im
        if half == 1:
            even.append((low_re + high_re, None))
            odd.append((cos * gap_re - sin * gap_im, None))
        else:
            even.append((low_re + high_re, low_im + high_im))
            odd.append((cos * gap_re - sin * gap_im, sin * gap_re + cos * gap_im))
    even, odd = split_inverse(even), split_inverse(odd)
    return [piece for pair in zip(even, odd) for piece in pair]


def mixer_kernel(
    lanes,
    groups,
    inner_hbm,
    values_hbm,
    outer_hbm,
    taps_hbm,
    skip_hbm,
    proj_ref,
    cos_hbm,
    sin_hbm,
    turn_cos_hbm,
    turn_sin_hbm,
    out_ref,
    inner_ref,
    values_ref,
    outer_ref,
    taps_ref,
    skip_ref,
    cos_ref,
    sin_ref,
    turn_cos_ref,
    turn_sin_ref,
    leave,
    arrive,
    sec_re,
    sec_im,
    back_re,
    back_im,
    conv_leave,
    conv_arrive,
    gathered,
    weights,
    total,
    in_send,
    in_recv,
    conv_send,
    conv_recv,
    side_send,
    side_recv,
    proj_send,
    proj_recv,
    proj_own,
    piece_sem,
    late_sem,
):
    me = lax.axis_index("seq")
    slab = lax.axis_index("chan")
    slabs = 4
    tokens = inner_ref.shape[0]
    wide = inner_ref.shape[1] // groups
    each = wide // lanes
    columns = out_ref.shape[1]
    sibling = slab + 1 - 2 * (slab % 2)
    across = (slab + 2) % 4
    corner = (sibling + 2) % 4

    def piece_copies(g):
        cols = pl.ds(pl.multiple_of(g * wide, wide), wide)
        pairs = ((inner_hbm, inner_ref), (values_hbm, values_ref), (taps_hbm, taps_ref))
        return [
            pltpu.make_async_copy(src.at[:, cols], dst.at[:, cols], piece_sem.at[g, i])
            for i, (src, dst) in enumerate(pairs)
        ]

    def late_copies(first, last):
        pairs = (
            (turn_cos_hbm, turn_cos_ref),
            (turn_sin_hbm, turn_sin_ref),
            (cos_hbm, cos_ref),
            (sin_hbm, sin_ref),
            (outer_hbm, outer_ref),
            (skip_hbm, skip_ref),
        )
        chosen = list(enumerate(pairs))[first:last]
        return [pltpu.make_async_copy(src, dst, late_sem.at[i]) for i, (src, dst) in chosen]

    for copy in piece_copies(0):
        copy.start()

    barrier = pltpu.get_barrier_semaphore()

    @pl.loop(1, lanes)
    def _(step):
        pl.semaphore_signal(
            barrier, inc=1, device_id={"seq": (me + step) % lanes}, device_id_type=MESH
        )

    for step in range(1, slabs):
        pl.semaphore_signal(
            barrier, inc=1, device_id={"chan": (slab + step) % slabs}, device_id_type=MESH
        )

    for g in range(1, groups):
        for copy in piece_copies(g):
            copy.start()

    def prepare(g):
        for copy in piece_copies(g):
            copy.wait()
        cols = pl.ds(pl.multiple_of(g * wide, wide), wide)
        mixed = inner_ref[:, cols].astype(jnp.float32) * values_ref[:, cols].astype(jnp.float32)
        mixed = mixed.T.astype(jnp.bfloat16)
        taps = taps_ref[:, cols].T.astype(jnp.bfloat16)
        for p in range(lanes):
            leave[g, p, 0] = mixed[p * each : (p + 1) * each, :]
            leave[g, p, 1] = taps[p * each : (p + 1) * each, :]
        arrive[g, me] = leave[g, me]

    def in_copy(g, step, source):
        target = (me + step) % lanes
        return pltpu.make_async_remote_copy(
            src_ref=leave.at[g, target],
            dst_ref=arrive.at[g, source],
            send_sem=in_send.at[g, step],
            recv_sem=in_recv.at[g, step],
            device_id={"seq": target},
            device_id_type=MESH,
        )

    def conv_copy(g, step, source):
        target = (me + step) % lanes
        return pltpu.make_async_remote_copy(
            src_ref=conv_leave.at[g, target],
            dst_ref=conv_arrive.at[g, source],
            send_sem=conv_send.at[g, step],
            recv_sem=conv_recv.at[g, step],
            device_id={"seq": target},
            device_id_type=MESH,
        )

    def proj_copy(step, source):
        target = (slab + step) % slabs
        return pltpu.make_async_remote_copy(
            src_ref=proj_ref.at[:, :, pl.ds(pl.multiple_of(target * columns, columns), columns)],
            dst_ref=weights.at[:, source],
            send_sem=proj_send.at[step],
            recv_sem=proj_recv.at[step],
            device_id={"chan": target},
            device_id_type=MESH,
        )

    def side_copy(g, kind, block, target):
        return pltpu.make_async_remote_copy(
            src_ref=gathered.at[g, block],
            dst_ref=gathered.at[g, block],
            send_sem=side_send.at[g, kind],
            recv_sem=side_recv.at[g, kind],
            device_id={"chan": target},
            device_id_type=MESH,
        )

    prepare(0)
    pl.semaphore_wait(barrier, lanes - 1 + slabs - 1)

    own_proj = pltpu.make_async_copy(
        proj_ref.at[:, :, pl.ds(pl.multiple_of(slab * columns, columns), columns)],
        weights.at[:, slab],
        proj_own,
    )

    @pl.loop(1, lanes)
    def _(step):
        in_copy(0, step, me).start()

    for copy in late_copies(0, 6):
        copy.start()
    own_proj.start()
    for step in range(1, slabs):
        proj_copy(step, slab).start()

    @pl.loop(1, groups)
    def _(g):
        prepare(g)

        @pl.loop(1, lanes)
        def _(step):
            in_copy(g, step, me).start()

    for copy in late_copies(0, 4):
        copy.wait()

    def dot(left, right):
        return jnp.dot(left, right, preferred_element_type=jnp.float32)

    @pl.loop(0, groups)
    def _(g):
        @pl.loop(1, lanes)
        def _(step):
            in_copy(g, step, (me + lanes - step) % lanes).wait_recv()

        @pl.loop(0, tokens // BLK)
        def _(j):
            span = pl.ds(pl.multiple_of(j * BLK, BLK), BLK)
            for sig in range(2):
                bins = split_forward(
                    [arrive[g, p, sig, :, span].astype(jnp.float32) for p in range(lanes)]
                )
                for k in range(lanes):
                    re, im = bins[k]
                    cos, sin = turn_cos_ref[k : k + 1, span], turn_sin_ref[k : k + 1, span]
                    sec_re[sig, k, :, span] = (re * cos + im * sin).astype(jnp.bfloat16)
                    sec_im[sig, k, :, span] = (im * cos - re * sin).astype(jnp.bfloat16)

        rows = lanes * each
        re = sec_re[...].reshape(2 * rows, tokens)
        im = sec_im[...].reshape(2 * rows, tokens)
        cos, sin = cos_ref[...], sin_ref[...]
        spec_re = dot(re, cos) + dot(im, sin)
        spec_im = dot(im, cos) - dot(re, sin)
        x_re, h_re = spec_re[:rows], spec_re[rows:]
        x_im, h_im = spec_im[:rows], spec_im[rows:]
        prod_re = (x_re * h_re - x_im * h_im).astype(jnp.bfloat16)
        prod_im = (x_re * h_im + x_im * h_re).astype(jnp.bfloat16)
        back_re[...] = (dot(prod_re, cos) - dot(prod_im, sin)).reshape(lanes, each, tokens)
        back_im[...] = (dot(prod_im, cos) + dot(prod_re, sin)).reshape(lanes, each, tokens)

        @pl.loop(0, tokens // BLK)
        def _(j):
            span = pl.ds(pl.multiple_of(j * BLK, BLK), BLK)
            bins = []
            for k in range(lanes):
                re, im = back_re[k, :, span], back_im[k, :, span]
                cos, sin = turn_cos_ref[k : k + 1, span], turn_sin_ref[k : k + 1, span]
                bins.append((re * cos - im * sin, re * sin + im * cos))
            pieces = split_inverse(bins)
            for p in range(lanes):
                conv_leave[g, p, :, span] = (pieces[p] * (1.0 / (lanes * tokens))).astype(
                    jnp.bfloat16
                )

        @pl.loop(1, lanes)
        def _(step):
            conv_copy(g, step, me).start()

        conv_arrive[g, me] = conv_leave[g, me]

    def forward(g):
        side_copy(g, 1, across, across).wait_recv()
        side_copy(g, 2, across, sibling).start()

    for copy in late_copies(4, 6):
        copy.wait()

    for g in range(groups):

        @pl.loop(1, lanes)
        def _(step):
            conv_copy(g, step, (me + lanes - step) % lanes).wait_recv()

        cols = slice(g * wide, (g + 1) * wide)
        conv = conv_arrive[g].astype(jnp.float32).reshape(wide, tokens).T
        gated = outer_ref[:, cols].astype(jnp.float32) * (
            conv + skip_ref[:, cols] * values_ref[:, cols].astype(jnp.float32)
        )
        gathered[g, slab] = gated.astype(jnp.bfloat16)
        side_copy(g, 1, slab, across).start()
        side_copy(g, 0, slab, sibling).start()
        if g > 0:
            forward(g - 1)
    forward(groups - 1)

    own_proj.wait()
    for step in range(1, slabs):
        proj_copy(step, (slab + slabs - step) % slabs).wait_recv()

    for g in range(groups):
        side_copy(g, 0, sibling, sibling).wait_recv()
        side_copy(g, 2, corner, sibling).wait_recv()
        left = jnp.concatenate([gathered[g, j] for j in range(slabs)], axis=1)
        part = dot(left, weights[g].reshape(slabs * wide, columns))
        if g == 0:
            total[...] = part
        elif g < groups - 1:
            total[...] += part
        else:
            out_ref[...] = (total[...] + part).astype(out_ref.dtype)

    @pl.loop(0, groups)
    def _(g):
        @pl.loop(1, lanes)
        def _(step):
            in_copy(g, step, me).wait_send()
            conv_copy(g, step, me).wait_send()

        side_copy(g, 0, slab, sibling).wait_send()
        side_copy(g, 1, slab, across).wait_send()
        side_copy(g, 2, across, sibling).wait_send()

    for step in range(1, slabs):
        proj_copy(step, slab).wait_send()


def kernel_on_device(lanes, groups, inner_gate, values, outer_gate, filter_taps, skip_gain, out_proj):
    slabs = 4
    tokens, channels = inner_gate.shape
    wide = channels // groups
    each = wide // lanes
    columns = out_proj.shape[1] // slabs
    index = np.arange(tokens)
    angles = 2.0 * np.pi * ((index[:, None] * index[None, :]) % tokens) / tokens
    turns = 2.0 * np.pi * (np.arange(lanes)[:, None] + SHIFT) * index[None, :] / (lanes * tokens)
    tables = (
        jnp.asarray(np.cos(angles), jnp.bfloat16),
        jnp.asarray(np.sin(angles), jnp.bfloat16),
        jnp.asarray(np.cos(turns), jnp.float32),
        jnp.asarray(np.sin(turns), jnp.float32),
    )
    here = pl.BlockSpec(memory_space=pltpu.VMEM)
    dma = pltpu.SemaphoreType.DMA
    return pl.pallas_call(
        functools.partial(mixer_kernel, lanes, groups),
        out_shape=jax.ShapeDtypeStruct((tokens, columns), jnp.bfloat16),
        in_specs=[pl.BlockSpec(memory_space=pltpu.HBM)] * 10,
        out_specs=here,
        scratch_shapes=[
            pltpu.VMEM((tokens, channels), jnp.bfloat16),
            pltpu.VMEM((tokens, channels), jnp.bfloat16),
            pltpu.VMEM((tokens, channels), jnp.bfloat16),
            pltpu.VMEM((tokens, channels), jnp.float32),
            pltpu.VMEM((1, channels), jnp.float32),
            pltpu.VMEM((tokens, tokens), jnp.bfloat16),
            pltpu.VMEM((tokens, tokens), jnp.bfloat16),
            pltpu.VMEM((lanes, tokens), jnp.float32),
            pltpu.VMEM((lanes, tokens), jnp.float32),
            pltpu.VMEM((groups, lanes, 2, each, tokens), jnp.bfloat16),
            pltpu.VMEM((groups, lanes, 2, each, tokens), jnp.bfloat16),
            pltpu.VMEM((2, lanes, each, tokens), jnp.bfloat16),
            pltpu.VMEM((2, lanes, each, tokens), jnp.bfloat16),
            pltpu.VMEM((lanes, each, tokens), jnp.float32),
            pltpu.VMEM((lanes, each, tokens), jnp.float32),
            pltpu.VMEM((groups, lanes, each, tokens), jnp.bfloat16),
            pltpu.VMEM((groups, lanes, each, tokens), jnp.bfloat16),
            pltpu.VMEM((groups, slabs, tokens, wide), jnp.bfloat16),
            pltpu.VMEM((groups, slabs, wide, columns), jnp.bfloat16),
            pltpu.VMEM((tokens, columns), jnp.float32),
            dma((groups, lanes)),
            dma((groups, lanes)),
            dma((groups, lanes)),
            dma((groups, lanes)),
            dma((groups, 3)),
            dma((groups, 3)),
            dma((slabs,)),
            dma((slabs,)),
            dma,
            dma((groups, 3)),
            dma((6,)),
        ],
        compiler_params=pltpu.CompilerParams(
            collective_id=0, has_side_effects=True, vmem_limit_bytes=63 * 1024 * 1024
        ),
    )(
        inner_gate,
        values,
        outer_gate,
        filter_taps,
        skip_gain.reshape(1, channels),
        out_proj.reshape(groups, wide, out_proj.shape[1]),
        *tables,
    )


def on_device(inner_gate, *others):
    lanes = lax.axis_size("seq")
    tokens, channels = inner_gate.shape
    groups = channels // (16 * lanes)
    fits = (
        lax.axis_size("chan") == 4
        and groups >= 2
        and channels == groups * 16 * lanes
        and lanes % 8 == 0
        and tokens % BLK == 0
        and lanes & (lanes - 1) == 0
    )
    if fits:
        return kernel_on_device(lanes, groups, inner_gate, *others)
    return plain_on_device(inner_gate, *others)


def solution(mesh):
    return jax.shard_map(
        on_device,
        mesh=mesh,
        in_specs=(
            P("seq", "chan"),
            P("seq", "chan"),
            P("seq", "chan"),
            P("seq", "chan"),
            P("chan"),
            P("chan", None),
        ),
        out_specs=P("seq", "chan"),
        check_vma=False,
    )
```

```python
import functools
import math

import jax
import jax.numpy as jnp
import numpy as np
from jax import lax
from jax.experimental import pallas as pl
from jax.experimental.pallas import tpu as pltpu
from jax.sharding import PartitionSpec as P

BLK = 128


def wave_table(length, direction):
    positions = jnp.arange(length, dtype=jnp.int32)
    phases = positions[:, None] * positions[None, :] % length
    angles = phases.astype(jnp.float32) * (2.0 * math.pi / length)
    return (
        jnp.cos(angles).astype(jnp.bfloat16),
        (direction * jnp.sin(angles)).astype(jnp.bfloat16),
    )


def twiddle(row_ids, col_ids, length, direction):
    phases = row_ids * col_ids % length
    angles = phases.astype(jnp.float32) * (2.0 * math.pi / length)
    return (jnp.cos(angles), direction * jnp.sin(angles))


def apply_table(pattern, table, signal):
    table_real, table_imag = table
    signal_real, signal_imag = signal
    out_real = jnp.einsum(pattern, table_real, signal_real, preferred_element_type=jnp.float32)
    out_imag = jnp.einsum(pattern, table_imag, signal_real, preferred_element_type=jnp.float32)
    if signal_imag is not None:
        out_real = out_real - jnp.einsum(
            pattern, table_imag, signal_imag, preferred_element_type=jnp.float32
        )
        out_imag = out_imag + jnp.einsum(
            pattern, table_real, signal_imag, preferred_element_type=jnp.float32
        )
    return (out_real, out_imag)


def twist_round(signal, factor):
    signal_real, signal_imag = signal
    factor_real, factor_imag = factor
    return (
        (signal_real * factor_real - signal_imag * factor_imag).astype(jnp.bfloat16),
        (signal_real * factor_imag + signal_imag * factor_real).astype(jnp.bfloat16),
    )


def lead_forward(signal, lane_table, first, tables, second):
    table_q, table_m = tables
    section = twist_round(apply_table("pk,cpqm->ckqm", lane_table, signal), first)
    shaped = twist_round(apply_table("qj,ckqm->ckjm", table_q, section), second)
    return apply_table("mn,ckjm->ckjn", table_m, shaped)


def lead_inverse(spectrum, tables, second, first):
    table_q, table_m = tables
    shaped = twist_round(apply_table("mn,ckjn->ckjm", table_m, spectrum), second)
    return twist_round(apply_table("qj,ckjm->ckqm", table_q, shaped), first)


def combine(even_part, odd_part, half_cos, half_sin, seq_length):
    return (even_part[0] + (half_cos * odd_part[0] - half_sin * odd_part[1])) / (2.0 * seq_length)


def plain_on_device(inner_gate, values, outer_gate, filter_taps, skip_gain, out_proj):
    seq_count = lax.axis_size("seq")
    my_index = lax.axis_index("seq")
    tokens = inner_gate.shape[0]
    seq_length = tokens * seq_count
    block_count = tokens // BLK
    forward_lane = wave_table(seq_count, -1.0)
    inverse_lane = wave_table(seq_count, 1.0)
    forward_local = (wave_table(block_count, -1.0), wave_table(BLK, -1.0))
    inverse_local = (wave_table(block_count, 1.0), wave_table(BLK, 1.0))
    own_angle = (my_index * tokens + jnp.arange(tokens, dtype=jnp.int32)).astype(
        jnp.float32
    ).reshape(tokens, 1) * (math.pi / seq_length)
    own_cos = jnp.cos(own_angle)
    own_sin = jnp.sin(own_angle)
    mixed = (inner_gate.astype(jnp.float32) * values.astype(jnp.float32)).astype(jnp.bfloat16)
    mixed = lax.optimization_barrier(mixed)
    mixed_wide = mixed.astype(jnp.float32)
    odd_real = (mixed_wide * own_cos).astype(jnp.bfloat16)
    odd_imag = (-(mixed_wide * own_sin)).astype(jnp.bfloat16)
    taps_even = filter_taps.astype(jnp.bfloat16)
    taps_real = (filter_taps * own_cos).astype(jnp.bfloat16)
    taps_imag = (-(filter_taps * own_sin)).astype(jnp.bfloat16)
    spread = (
        lax.all_to_all(mixed, "seq", split_axis=1, concat_axis=0, tiled=True),
        lax.all_to_all(odd_real, "seq", split_axis=1, concat_axis=0, tiled=True),
        lax.all_to_all(odd_imag, "seq", split_axis=1, concat_axis=0, tiled=True),
        lax.all_to_all(taps_even, "seq", split_axis=1, concat_axis=0, tiled=True),
        lax.all_to_all(taps_real, "seq", split_axis=1, concat_axis=0, tiled=True),
        lax.all_to_all(taps_imag, "seq", split_axis=1, concat_axis=0, tiled=True),
    )
    slab_width = spread[0].shape[1]
    slabs = [piece.T.reshape(slab_width, seq_count, block_count, BLK) for piece in spread]
    outer_flat = jnp.arange(block_count, dtype=jnp.int32).reshape(block_count, 1)
    inner_flat = jnp.arange(BLK, dtype=jnp.int32).reshape(1, BLK)
    second_forward = twiddle(outer_flat, inner_flat, tokens, -1.0)
    second_inverse = twiddle(outer_flat, inner_flat, tokens, 1.0)
    lane_index = jnp.arange(seq_count, dtype=jnp.int32).reshape(seq_count, 1, 1)
    row_index = jnp.arange(tokens, dtype=jnp.int32).reshape(1, block_count, BLK)
    first_forward = twiddle(lane_index, row_index, seq_length, -1.0)
    first_inverse = twiddle(lane_index, row_index, seq_length, 1.0)
    signals = ((slabs[0], None), (slabs[1], slabs[2]), (slabs[3], None), (slabs[4], slabs[5]))
    spectra = [
        lead_forward(signal, forward_lane, first_forward, forward_local, second_forward)
        for signal in signals
    ]
    product_even = twist_round(spectra[0], spectra[2])
    product_odd = twist_round(spectra[1], spectra[3])
    back_even = lead_inverse(product_even, inverse_local, second_inverse, first_inverse)
    back_odd = lead_inverse(product_odd, inverse_local, second_inverse, first_inverse)
    even_part = apply_table("pk,ckqm->cpqm", inverse_lane, back_even)
    odd_part = apply_table("pk,ckqm->cpqm", inverse_lane, back_odd)
    lane_angle = (lane_index * tokens + row_index).astype(jnp.float32) * (math.pi / seq_length)
    slab_conv = combine(even_part, odd_part, jnp.cos(lane_angle), jnp.sin(lane_angle), seq_length)
    slab_conv = slab_conv.reshape(slab_width, seq_length).T
    convolved = lax.all_to_all(
        slab_conv.astype(jnp.bfloat16), "seq", split_axis=0, concat_axis=1, tiled=True
    ).astype(slab_conv.dtype)
    gated = (
        outer_gate.astype(jnp.float32)
        * (convolved + skip_gain[None, :] * values.astype(jnp.float32))
    ).astype(jnp.bfloat16)
    partial_value = jnp.dot(gated, out_proj, preferred_element_type=jnp.float32)
    return lax.psum_scatter(
        partial_value.astype(jnp.bfloat16), "chan", scatter_dimension=1, tiled=True
    )


SHIFT = 0.25
MESH = pl.DeviceIdType.MESH


def split_forward(pieces):
    count = len(pieces)
    if count == 1:
        return [(pieces[0], None)]
    even, odd = split_forward(pieces[0::2]), split_forward(pieces[1::2])
    low, high = [], []
    for k in range(count // 2):
        angle = 2.0 * math.pi * (k + SHIFT) / count
        cos, sin = math.cos(angle), math.sin(angle)
        odd_re, odd_im = odd[k]
        even_re, even_im = even[k]
        if odd_im is None:
            turn_re, turn_im = cos * odd_re, -sin * odd_re
            low.append((even_re + turn_re, turn_im))
            high.append((even_re - turn_re, -turn_im))
        else:
            turn_re = cos * odd_re + sin * odd_im
            turn_im = cos * odd_im - sin * odd_re
            low.append((even_re + turn_re, even_im + turn_im))
            high.append((even_re - turn_re, even_im - turn_im))
    return low + high


def split_inverse(bins):
    count = len(bins)
    if count == 1:
        return [bins[0][0]]
    half = count // 2
    even, odd = [], []
    for k in range(half):
        angle = 2.0 * math.pi * (k + SHIFT) / count
        cos, sin = math.cos(angle), math.sin(angle)
        (low_re, low_im), (high_re, high_im) = bins[k], bins[k + half]
        gap_re, gap_im = low_re - high_re, low_im - high_im
        if half == 1:
            even.append((low_re + high_re, None))
            odd.append((cos * gap_re - sin * gap_im, None))
        else:
            even.append((low_re + high_re, low_im + high_im))
            odd.append((cos * gap_re - sin * gap_im, sin * gap_re + cos * gap_im))
    even, odd = split_inverse(even), split_inverse(odd)
    return [piece for pair in zip(even, odd) for piece in pair]


def mixer_kernel(
    lanes,
    groups,
    inner_hbm,
    values_hbm,
    outer_hbm,
    taps_hbm,
    skip_hbm,
    proj_ref,
    cos_hbm,
    sin_hbm,
    turn_cos_hbm,
    turn_sin_hbm,
    out_ref,
    inner_ref,
    values_ref,
    outer_ref,
    taps_ref,
    skip_ref,
    cos_ref,
    sin_ref,
    turn_cos_ref,
    turn_sin_ref,
    leave,
    arrive,
    sec_re,
    sec_im,
    back_re,
    back_im,
    conv_leave,
    conv_arrive,
    gathered,
    weights,
    total,
    in_send,
    in_recv,
    conv_send,
    conv_recv,
    side_send,
    side_recv,
    proj_send,
    proj_recv,
    proj_own,
    piece_sem,
    late_sem,
):
    me = lax.axis_index("seq")
    slab = lax.axis_index("chan")
    slabs = 4
    tokens = inner_ref.shape[0]
    wide = inner_ref.shape[1] // groups
    each = wide // lanes
    columns = out_ref.shape[1]
    sibling = slab + 1 - 2 * (slab % 2)
    across = (slab + 2) % 4
    corner = (sibling + 2) % 4

    def piece_copies(g):
        cols = pl.ds(pl.multiple_of(g * wide, wide), wide)
        pairs = ((inner_hbm, inner_ref), (values_hbm, values_ref), (taps_hbm, taps_ref))
        return [
            pltpu.make_async_copy(src.at[:, cols], dst.at[:, cols], piece_sem.at[g, i])
            for i, (src, dst) in enumerate(pairs)
        ]

    def late_copies(first, last):
        pairs = (
            (turn_cos_hbm, turn_cos_ref),
            (turn_sin_hbm, turn_sin_ref),
            (cos_hbm, cos_ref),
            (sin_hbm, sin_ref),
            (outer_hbm, outer_ref),
            (skip_hbm, skip_ref),
        )
        chosen = list(enumerate(pairs))[first:last]
        return [pltpu.make_async_copy(src, dst, late_sem.at[i]) for i, (src, dst) in chosen]

    for copy in piece_copies(0):
        copy.start()

    barrier = pltpu.get_barrier_semaphore()

    @pl.loop(1, lanes)
    def _(step):
        pl.semaphore_signal(
            barrier, inc=1, device_id={"seq": (me + step) % lanes}, device_id_type=MESH
        )

    for step in range(1, slabs):
        pl.semaphore_signal(
            barrier, inc=1, device_id={"chan": (slab + step) % slabs}, device_id_type=MESH
        )

    for g in range(1, groups):
        for copy in piece_copies(g):
            copy.start()

    def spread(send):
        half = lanes // 2

        @pl.loop(0, lanes - 1)
        def _(i):
            send(half + (1 - 2 * (i % 2)) * ((i + 1) // 2))

    def prepare(g):
        for copy in piece_copies(g):
            copy.wait()
        cols = pl.ds(pl.multiple_of(g * wide, wide), wide)
        mixed = inner_ref[:, cols].astype(jnp.float32) * values_ref[:, cols].astype(jnp.float32)
        mixed = mixed.T.astype(jnp.bfloat16)
        taps = taps_ref[:, cols].T.astype(jnp.bfloat16)
        for p in range(lanes):
            leave[g, p, 0] = mixed[p * each : (p + 1) * each, :]
            leave[g, p, 1] = taps[p * each : (p + 1) * each, :]
        arrive[g, me] = leave[g, me]

    def in_copy(g, step, source):
        target = (me + step) % lanes
        return pltpu.make_async_remote_copy(
            src_ref=leave.at[g, target],
            dst_ref=arrive.at[g, source],
            send_sem=in_send.at[g, step],
            recv_sem=in_recv.at[g, step],
            device_id={"seq": target},
            device_id_type=MESH,
        )

    def conv_copy(g, step, source):
        target = (me + step) % lanes
        return pltpu.make_async_remote_copy(
            src_ref=conv_leave.at[g, target],
            dst_ref=conv_arrive.at[g, source],
            send_sem=conv_send.at[g, step],
            recv_sem=conv_recv.at[g, step],
            device_id={"seq": target},
            device_id_type=MESH,
        )

    def proj_copy(step, source):
        target = (slab + step) % slabs
        return pltpu.make_async_remote_copy(
            src_ref=proj_ref.at[:, :, pl.ds(pl.multiple_of(target * columns, columns), columns)],
            dst_ref=weights.at[:, source],
            send_sem=proj_send.at[step],
            recv_sem=proj_recv.at[step],
            device_id={"chan": target},
            device_id_type=MESH,
        )

    def side_copy(g, kind, block, target):
        return pltpu.make_async_remote_copy(
            src_ref=gathered.at[g, block],
            dst_ref=gathered.at[g, block],
            send_sem=side_send.at[g, kind],
            recv_sem=side_recv.at[g, kind],
            device_id={"chan": target},
            device_id_type=MESH,
        )

    prepare(0)
    pl.semaphore_wait(barrier, lanes - 1 + slabs - 1)

    own_proj = pltpu.make_async_copy(
        proj_ref.at[:, :, pl.ds(pl.multiple_of(slab * columns, columns), columns)],
        weights.at[:, slab],
        proj_own,
    )

    spread(lambda step: in_copy(0, step, me).start())

    for copy in late_copies(0, 6):
        copy.start()
    own_proj.start()
    for step in range(1, slabs):
        proj_copy(step, slab).start()

    @pl.loop(1, groups)
    def _(g):
        prepare(g)

        spread(lambda step: in_copy(g, step, me).start())

    for copy in late_copies(0, 4):
        copy.wait()

    def dot(left, right):
        return jnp.dot(left, right, preferred_element_type=jnp.float32)

    @pl.loop(0, groups)
    def _(g):
        @pl.loop(1, lanes)
        def _(step):
            in_copy(g, step, (me + lanes - step) % lanes).wait_recv()

        @pl.loop(0, tokens // BLK)
        def _(j):
            span = pl.ds(pl.multiple_of(j * BLK, BLK), BLK)
            for sig in range(2):
                bins = split_forward(
                    [arrive[g, p, sig, :, span].astype(jnp.float32) for p in range(lanes)]
                )
                for k in range(lanes):
                    re, im = bins[k]
                    cos, sin = turn_cos_ref[k : k + 1, span], turn_sin_ref[k : k + 1, span]
                    sec_re[sig, k, :, span] = (re * cos + im * sin).astype(jnp.bfloat16)
                    sec_im[sig, k, :, span] = (im * cos - re * sin).astype(jnp.bfloat16)

        rows = lanes * each
        re = sec_re[...].reshape(2 * rows, tokens)
        im = sec_im[...].reshape(2 * rows, tokens)
        cos, sin = cos_ref[...], sin_ref[...]
        spec_re = dot(re, cos) + dot(im, sin)
        spec_im = dot(im, cos) - dot(re, sin)
        x_re, h_re = spec_re[:rows], spec_re[rows:]
        x_im, h_im = spec_im[:rows], spec_im[rows:]
        prod_re = (x_re * h_re - x_im * h_im).astype(jnp.bfloat16)
        prod_im = (x_re * h_im + x_im * h_re).astype(jnp.bfloat16)
        back_re[...] = (dot(prod_re, cos) - dot(prod_im, sin)).reshape(lanes, each, tokens)
        back_im[...] = (dot(prod_im, cos) + dot(prod_re, sin)).reshape(lanes, each, tokens)

        @pl.loop(0, tokens // BLK)
        def _(j):
            span = pl.ds(pl.multiple_of(j * BLK, BLK), BLK)
            bins = []
            for k in range(lanes):
                re, im = back_re[k, :, span], back_im[k, :, span]
                cos, sin = turn_cos_ref[k : k + 1, span], turn_sin_ref[k : k + 1, span]
                bins.append((re * cos - im * sin, re * sin + im * cos))
            pieces = split_inverse(bins)
            for p in range(lanes):
                conv_leave[g, p, :, span] = (pieces[p] * (1.0 / (lanes * tokens))).astype(
                    jnp.bfloat16
                )

        spread(lambda step: conv_copy(g, step, me).start())

        conv_arrive[g, me] = conv_leave[g, me]

    def forward(g):
        side_copy(g, 1, across, across).wait_recv()
        side_copy(g, 2, across, sibling).start()

    def project(g):
        side_copy(g, 0, sibling, sibling).wait_recv()
        side_copy(g, 2, corner, sibling).wait_recv()
        left = jnp.concatenate([gathered[g, j] for j in range(slabs)], axis=1)
        part = dot(left, weights[g].reshape(slabs * wide, columns))
        if g == 0:
            total[...] = part
        elif g < groups - 1:
            total[...] += part
        else:
            out_ref[...] = (total[...] + part).astype(out_ref.dtype)

    for copy in late_copies(4, 6):
        copy.wait()
    own_proj.wait()
    for step in range(1, slabs):
        proj_copy(step, (slab + slabs - step) % slabs).wait_recv()

    for g in range(groups):

        @pl.loop(1, lanes)
        def _(step):
            conv_copy(g, step, (me + lanes - step) % lanes).wait_recv()

        cols = slice(g * wide, (g + 1) * wide)
        conv = conv_arrive[g].astype(jnp.float32).reshape(wide, tokens).T
        gated = outer_ref[:, cols].astype(jnp.float32) * (
            conv + skip_ref[:, cols] * values_ref[:, cols].astype(jnp.float32)
        )
        gathered[g, slab] = gated.astype(jnp.bfloat16)
        side_copy(g, 1, slab, across).start()
        side_copy(g, 0, slab, sibling).start()
        if g > 0:
            forward(g - 1)
        if g > 1:
            project(g - 2)
    project(groups - 2)
    forward(groups - 1)
    project(groups - 1)

    @pl.loop(0, groups)
    def _(g):
        @pl.loop(1, lanes)
        def _(step):
            in_copy(g, step, me).wait_send()
            conv_copy(g, step, me).wait_send()

        side_copy(g, 0, slab, sibling).wait_send()
        side_copy(g, 1, slab, across).wait_send()
        side_copy(g, 2, across, sibling).wait_send()

    for step in range(1, slabs):
        proj_copy(step, slab).wait_send()


def kernel_on_device(lanes, groups, inner_gate, values, outer_gate, filter_taps, skip_gain, out_proj):
    slabs = 4
    tokens, channels = inner_gate.shape
    wide = channels // groups
    each = wide // lanes
    columns = out_proj.shape[1] // slabs
    index = np.arange(tokens)
    angles = 2.0 * np.pi * ((index[:, None] * index[None, :]) % tokens) / tokens
    turns = 2.0 * np.pi * (np.arange(lanes)[:, None] + SHIFT) * index[None, :] / (lanes * tokens)
    tables = (
        jnp.asarray(np.cos(angles), jnp.bfloat16),
        jnp.asarray(np.sin(angles), jnp.bfloat16),
        jnp.asarray(np.cos(turns), jnp.float32),
        jnp.asarray(np.sin(turns), jnp.float32),
    )
    here = pl.BlockSpec(memory_space=pltpu.VMEM)
    dma = pltpu.SemaphoreType.DMA
    return pl.pallas_call(
        functools.partial(mixer_kernel, lanes, groups),
        out_shape=jax.ShapeDtypeStruct((tokens, columns), jnp.bfloat16),
        in_specs=[pl.BlockSpec(memory_space=pltpu.HBM)] * 10,
        out_specs=here,
        scratch_shapes=[
            pltpu.VMEM((tokens, channels), jnp.bfloat16),
            pltpu.VMEM((tokens, channels), jnp.bfloat16),
            pltpu.VMEM((tokens, channels), jnp.bfloat16),
            pltpu.VMEM((tokens, channels), jnp.float32),
            pltpu.VMEM((1, channels), jnp.float32),
            pltpu.VMEM((tokens, tokens), jnp.bfloat16),
            pltpu.VMEM((tokens, tokens), jnp.bfloat16),
            pltpu.VMEM((lanes, tokens), jnp.float32),
            pltpu.VMEM((lanes, tokens), jnp.float32),
            pltpu.VMEM((groups, lanes, 2, each, tokens), jnp.bfloat16),
            pltpu.VMEM((groups, lanes, 2, each, tokens), jnp.bfloat16),
            pltpu.VMEM((2, lanes, each, tokens), jnp.bfloat16),
            pltpu.VMEM((2, lanes, each, tokens), jnp.bfloat16),
            pltpu.VMEM((lanes, each, tokens), jnp.float32),
            pltpu.VMEM((lanes, each, tokens), jnp.float32),
            pltpu.VMEM((groups, lanes, each, tokens), jnp.bfloat16),
            pltpu.VMEM((groups, lanes, each, tokens), jnp.bfloat16),
            pltpu.VMEM((groups, slabs, tokens, wide), jnp.bfloat16),
            pltpu.VMEM((groups, slabs, wide, columns), jnp.bfloat16),
            pltpu.VMEM((tokens, columns), jnp.float32),
            dma((groups, lanes)),
            dma((groups, lanes)),
            dma((groups, lanes)),
            dma((groups, lanes)),
            dma((groups, 3)),
            dma((groups, 3)),
            dma((slabs,)),
            dma((slabs,)),
            dma,
            dma((groups, 3)),
            dma((6,)),
        ],
        compiler_params=pltpu.CompilerParams(
            collective_id=0, has_side_effects=True, vmem_limit_bytes=63 * 1024 * 1024
        ),
    )(
        inner_gate,
        values,
        outer_gate,
        filter_taps,
        skip_gain.reshape(1, channels),
        out_proj.reshape(groups, wide, out_proj.shape[1]),
        *tables,
    )


def on_device(inner_gate, *others):
    lanes = lax.axis_size("seq")
    tokens, channels = inner_gate.shape
    groups = channels // (16 * lanes)
    fits = (
        lax.axis_size("chan") == 4
        and groups >= 2
        and channels == groups * 16 * lanes
        and lanes % 8 == 0
        and tokens % BLK == 0
        and lanes & (lanes - 1) == 0
    )
    if fits:
        return kernel_on_device(lanes, groups, inner_gate, *others)
    return plain_on_device(inner_gate, *others)


def solution(mesh):
    return jax.shard_map(
        on_device,
        mesh=mesh,
        in_specs=(
            P("seq", "chan"),
            P("seq", "chan"),
            P("seq", "chan"),
            P("seq", "chan"),
            P("chan"),
            P("chan", None),
        ),
        out_specs=P("seq", "chan"),
        check_vma=False,
    )
```
